256 devices in a mesh: section: 8 (over y_lo, x), seq: 32 (over y_hi, z, core).
Axes of the slice: x: 4, y: 4 (y_hi: 2, y_lo: 2; y = y_hi * 2 + y_lo), z: 8, core: 2. Of those that a mesh axis runs over, the one named last changes fastest.
Arguments:
- stream: bfloat16 [8, 4096, 3584], P('section', 'seq'), may hold values from -6 to 6
- keys: bfloat16 [8, 4096, 3584], P('section', 'seq'), may hold values from -400 to 400
- values: bfloat16 [8, 4096, 3584], P('section', 'seq'), may hold values from -6 to 6
- bc: bfloat16 [8, 4096, 128], P('section', 'seq'), may hold values from -3 to 3
- rates: float32 [8, 4096, 56], P('section', 'seq'), may hold values from 0 to 1, as said below
- dskip: float32 [8, 56], P('section'), may hold values from 1 to 8
- norm_gain: float32 [8, 3584], P('section'), may hold values from 0.25 to 1.75
- seg_ids: int32 [8, 4096], P('section', 'seq'), may hold values from 0 to 31, never falling along the last dimension, each value on 1 to 512 neighbouring positions
Outputs:
- next_stream: bfloat16 [8, 4096, 3584], P('section', 'seq')
The draws below stay inside these ranges and needn't reach their ends.
Inputs may be any that keep to these rules, and one draw needn't show every extreme that they name: `seg_ids`: each document covers at most 512 consecutive positions, and in every row some document covers exactly that many. `rates`: Positive.
All inputs are finite; a program needn't handle non-finite values.
Results may differ from the reference program's by a relative error of at most 0.0085.
Values may be sent and summed in bfloat16 or wider, within the bound.
A program may use at most 128 MiB of HBM per device.

```python
import math
import jax
import jax.numpy as jnp
import numpy as np
from jax import lax

SSD_ATTN_GROUPS = 56
HEAD_P = 64
NSTATE = 64
ATT_HEADS = 16
ATT_DIM = 224
ROWS = 128
BACK = 4
HIDDEN_W = 3584
CHAIN_PORTIONS = 8
TOKEN_POSITIONS = 4096
N_SEQ = 32


def draw_keys(key, part):
    key = jax.random.fold_in(key, 11)
    first = jax.random.fold_in(key, 0)
    starting_level = jnp.clip(jax.random.normal(first, (CHAIN_PORTIONS, TOKEN_POSITIONS, HIDDEN_W), jnp.float32), -8.0, 8.0)
    return starting_level.astype(jnp.bfloat16)


def draw_rates(key, part):
    key = jax.random.fold_in(key, 23)
    gradual_random_seed, floor_random_seed, quick_random_seed, jitter_random_seed, spike_random_seed, extent_random_seed = jax.random.split(key, 6)
    slow_share = 0.5
    slow = jax.random.uniform(gradual_random_seed, (CHAIN_PORTIONS, 1, SSD_ATTN_GROUPS), jnp.float32) < slow_share
    slow_rate = jnp.exp(jax.random.uniform(floor_random_seed, (CHAIN_PORTIONS, 1, SSD_ATTN_GROUPS), jnp.float32, math.log(0.1), math.log(0.8))) / TOKEN_POSITIONS
    fast_rate = jnp.exp(jax.random.uniform(quick_random_seed, (CHAIN_PORTIONS, 1, SSD_ATTN_GROUPS), jnp.float32, math.log(1.0 / 50.0), math.log(1.0 / 30.0)))
    starting_level = jnp.where(slow, slow_rate, fast_rate)
    jitter_perturbation = jax.random.uniform(jitter_random_seed, (CHAIN_PORTIONS, TOKEN_POSITIONS, SSD_ATTN_GROUPS), jnp.float32, 0.5, 1.5)
    spike_magnitude = jax.random.uniform(spike_random_seed, (CHAIN_PORTIONS, TOKEN_POSITIONS, SSD_ATTN_GROUPS), jnp.float32) < 2.0 / TOKEN_POSITIONS
    extent_sample = jax.random.uniform(extent_random_seed, (CHAIN_PORTIONS, TOKEN_POSITIONS, SSD_ATTN_GROUPS), jnp.float32, 0.2, 0.7)
    return starting_level * jitter_perturbation + jnp.where(spike_magnitude, extent_sample, 0.0)


def steps_of(own_key, dims, cuts, low, largest):
    loudness, own = 1.0, jax.random.fold_in(own_key, 6)
    for position, parts in cuts:
        heights = jnp.exp(jax.random.uniform(jax.random.fold_in(own, position), (parts,), jnp.float32, low / len(cuts), largest / len(cuts)))
        loudness = loudness * jnp.repeat(heights, dims[position] // parts).reshape([-1 if axis == position else 1 for axis in range(len(dims))])
    return loudness


def length_profile(count, total, most, slope):
    loads = [(1 << 20) // math.isqrt(rank ** slope) + 1 for rank in range(2, count + 1)]
    spare, counts = total - most - (count - 1), [1] * (count - 1)
    while spare > 0:
        movable = [i for i in range(count - 1) if counts[i] < most]
        pool, remaining = sum([loads[i] for i in movable]), spare
        for i in movable:
            addition = min(most - counts[i], max(1, remaining * loads[i] // pool), spare)
            counts[i] = counts[i] + addition
            spare = spare - addition
    return np.array([most] + counts)


def ragged_sizes(key, number_of, total, limit, skew):
    if number_of == 2:
        one = jax.random.randint(key, (), max(1, total - limit), min(limit, total - 1) + 1)
        return jnp.stack([one, total - one])
    sizes = jnp.asarray(length_profile(number_of, total, limit, skew), jnp.int32)
    pairs = (number_of - 1) // 2
    donor, receiver = sizes[1:1 + 2 * pairs:2], sizes[2:2 + 2 * pairs:2]
    slack = jnp.minimum(donor - 1, limit - receiver)
    passed = jax.random.randint(jax.random.fold_in(key, 1), (pairs,), 0, 1 << 20) % (slack + 1)
    sizes = sizes.at[1:1 + 2 * pairs:2].set(donor - passed).at[2:2 + 2 * pairs:2].set(receiver + passed)
    return sizes[jax.random.permutation(jax.random.fold_in(key, 2), number_of)]


def centred(key, dims, spread, reach, pieces=(), kind=jnp.bfloat16):
    level = steps_of(key, dims, pieces, -0.22, 0.18) if pieces else 1.0
    result = jax.random.normal(key, dims, jnp.float32) * spread * level
    return jnp.minimum(jnp.maximum(result, -reach), reach).astype(kind)


def setup_inputs(seed: int = 0) -> dict:
    seeds = jax.random.split(jax.random.key(seed), 9)
    return {
        "stream": centred(seeds[0], (CHAIN_PORTIONS, TOKEN_POSITIONS, HIDDEN_W), 1.0, 6.0, ((0, 8), (1, 32))),
        "keys": draw_keys(jax.random.fold_in(seeds[8], 71), 0),
        "values": centred(seeds[2], (CHAIN_PORTIONS, TOKEN_POSITIONS, HIDDEN_W), 1.0, 6.0, ((0, 8), (1, 32))),
        "bc": centred(seeds[3], (CHAIN_PORTIONS, TOKEN_POSITIONS, 2 * NSTATE), 0.36, 3.0, ((0, 8), (1, 32))),
        "rates": draw_rates(jax.random.fold_in(seeds[8], 71), 0),
        "dskip": jnp.clip(jnp.exp(math.log(8.0) - 2.0794415 * jax.random.uniform(seeds[5], (CHAIN_PORTIONS, SSD_ATTN_GROUPS), jnp.float32) ** steps_of(seeds[5], (CHAIN_PORTIONS, SSD_ATTN_GROUPS), ((0, 8),), -0.2, 0.2)), 1.0, 8.0),
        "norm_gain": jnp.clip(1.0 + 0.15 * jax.random.normal(seeds[6], (CHAIN_PORTIONS, HIDDEN_W), jnp.float32), 0.25, 1.75),
        "seg_ids": jax.vmap(lambda own: jnp.searchsorted(jnp.cumsum(ragged_sizes(own, TOKEN_POSITIONS // ROWS, TOKEN_POSITIONS, BACK * ROWS, 2)), jnp.arange(TOKEN_POSITIONS), side="right"))(jax.random.split(seeds[7], CHAIN_PORTIONS)).reshape((CHAIN_PORTIONS, TOKEN_POSITIONS)).astype(jnp.int32),
    }


def mixer(x, bc, rates, dskip, gain, state_in):
    rows = x.shape[0]
    xh = x.reshape(rows, SSD_ATTN_GROUPS, HEAD_P)
    bmat = bc[:, :NSTATE]
    cmat = bc[:, NSTATE:]
    cum = jnp.cumsum(rates, axis=0)
    total = cum[-1]
    inner_dot = jnp.dot(cmat, bmat.T, preferred_element_type=jnp.float32)
    cum_t = cum.T
    gap = cum_t[:, :, None] - cum_t[:, None, :]
    lower = jnp.arange(rows)[:, None] >= jnp.arange(rows)[None, :]
    decay = jnp.where(lower[None], jnp.exp(-jnp.where(lower[None], gap, 0.0)), 0.0)
    mixing = (inner_dot[None] * decay).astype(jnp.bfloat16)
    inner = jnp.einsum('hts,shp->thp', mixing.astype(jnp.float32), xh.astype(jnp.float32))
    flat_state = state_in.reshape(HIDDEN_W, NSTATE)
    carried = jnp.dot(cmat.astype(jnp.float32), flat_state.T, precision=lax.Precision.HIGHEST)
    carried = carried.reshape(rows, SSD_ATTN_GROUPS, HEAD_P) * jnp.exp(-cum)[:, :, None]
    y_full = inner + carried + dskip[None, :, None] * xh.astype(jnp.float32)
    meansq = lax.optimization_barrier(jnp.mean(y_full * y_full, axis=-1, keepdims=True))
    normed = (y_full * lax.rsqrt(meansq + 1e-05)).reshape(rows, HIDDEN_W) * gain[None, :]
    u_out = normed.astype(jnp.bfloat16)
    weight = jnp.exp(-(total[None, :] - cum))
    weighted = (xh.astype(jnp.float32) * weight[:, :, None]).reshape(rows, HIDDEN_W)
    local = jnp.dot(weighted.T, bmat.astype(jnp.float32), precision=lax.Precision.HIGHEST)
    return (u_out, jnp.exp(-total), local.reshape(SSD_ATTN_GROUPS, HEAD_P * NSTATE))

def attend(u_rows, keys_win, values_win, seg_q, seg_k, qpos, kpos):
    rows = u_rows.shape[0]
    query = u_rows.reshape(rows, ATT_HEADS, ATT_DIM).astype(jnp.float32)
    key_h = keys_win.reshape(-1, ATT_HEADS, ATT_DIM).astype(jnp.float32)
    val_h = values_win.reshape(-1, ATT_HEADS, ATT_DIM).astype(jnp.float32)
    scores = jnp.einsum('thd,khd->htk', query, key_h) * ATT_DIM ** (-0.5)
    allowed = (kpos[None, :] >= 0) & (kpos[None, :] <= qpos[:, None]) & (seg_k[None, :] == seg_q[:, None])
    scores = jnp.where(allowed[None], scores, -1e+30)
    top = lax.optimization_barrier(jnp.max(scores, axis=-1, keepdims=True))
    expo = jnp.where(allowed[None], jnp.exp(scores - top), 0.0)
    totals = lax.optimization_barrier(jnp.sum(expo, axis=-1))
    probs = expo.astype(jnp.bfloat16)
    attended = jnp.einsum('htk,khd->thd', probs.astype(jnp.float32), val_h) / totals.T[:, :, None]
    return attended.reshape(rows, HIDDEN_W)

def one_section(pack):
    stream, keys, values, bc, rates, dskip, gain, seg_ids = pack
    blocks = N_SEQ
    xb = stream.reshape(blocks, ROWS, HIDDEN_W)
    bcb = bc.reshape(blocks, ROWS, 2 * NSTATE)
    rb = rates.reshape(blocks, ROWS, SSD_ATTN_GROUPS)

    def step(state, item):
        xrow, bcrow, rrow = item
        u_out, dtot, local = mixer(xrow, bcrow, rrow, dskip, gain, state)
        return (dtot[:, None] * state + local, u_out)
    start_state = jnp.zeros((SSD_ATTN_GROUPS, HEAD_P * NSTATE), jnp.float32)
    _, u_blocks = lax.scan(step, start_state, (xb, bcb, rb))
    u_all = u_blocks.reshape(TOKEN_POSITIONS, HIDDEN_W)
    keys_pad = jnp.concatenate([jnp.zeros((BACK * ROWS, HIDDEN_W), jnp.bfloat16), keys], axis=0)
    values_pad = jnp.concatenate([jnp.zeros((BACK * ROWS, HIDDEN_W), jnp.bfloat16), values], axis=0)
    seg_pad = jnp.concatenate([jnp.full((BACK * ROWS,), -1, jnp.int32), seg_ids.astype(jnp.int32)], axis=0)

    def attend_block(block):
        start = (block * ROWS).astype(jnp.int32)
        u_rows = lax.dynamic_slice_in_dim(u_all, start, ROWS)
        x_rows = lax.dynamic_slice_in_dim(stream, start, ROWS)
        seg_q = lax.dynamic_slice_in_dim(seg_ids.astype(jnp.int32), start, ROWS)
        keys_win = lax.dynamic_slice_in_dim(keys_pad, start, (BACK + 1) * ROWS)
        values_win = lax.dynamic_slice_in_dim(values_pad, start, (BACK + 1) * ROWS)
        seg_k = lax.dynamic_slice_in_dim(seg_pad, start, (BACK + 1) * ROWS)
        qpos = start + jnp.arange(ROWS, dtype=jnp.int32)
        kpos = start - BACK * ROWS + jnp.arange((BACK + 1) * ROWS, dtype=jnp.int32)
        attended = attend(u_rows, keys_win, values_win, seg_q, seg_k, qpos, kpos)
        summed = x_rows.astype(jnp.float32) + u_rows.astype(jnp.float32) + attended
        return summed.astype(jnp.bfloat16)
    outs = lax.map(attend_block, jnp.arange(blocks, dtype=jnp.int32))
    return outs.reshape(TOKEN_POSITIONS, HIDDEN_W)

def reference(stream, keys, values, bc, rates, dskip, norm_gain, seg_ids):
    outs = lax.map(one_section, (stream, keys, values, bc, rates, dskip, norm_gain, seg_ids))
    return jnp.roll(outs, 1, axis=0)
```

```python
import functools

import jax
import jax.numpy as jnp
from jax import lax
from jax.experimental import pallas as pl
from jax.experimental.pallas import tpu as pltpu
from jax.sharding import PartitionSpec as P

ROWS = 128
HEAD_P = 64
NSTATE = 64
ATT_DIM = 224
BACK = 4
LANES = 128
QUAD = 4 * ATT_DIM
TILES = QUAD // LANES
SPAN = (BACK + 1) * ROWS
LOWEST = -1e20
MASKED = -1e30
WINDOWS = ((0, 256), (128, 384), (384, 384), (640, 256))
MODES = ("q", "q", "q", "k")
MESH = pl.DeviceIdType.MESH
F32 = jnp.float32
BF16 = jnp.bfloat16


def iota(shape, dim):
    return lax.broadcasted_iota(jnp.int32, shape, dim)


def halves(a):
    hi = a.astype(BF16)
    return hi, (a - hi.astype(F32)).astype(BF16)


def dot(a, b, dims=((1,), (0,)), precision=None):
    return lax.dot_general(a, b, (dims, ((), ())), precision=precision, preferred_element_type=F32)


def kernel(
    modes, sections, peers,
    x_ref, k_ref, v_ref, bc_ref, rate_ref, dskip_ref, gain_ref, seg_ref,
    out_ref,
    cumx, y0, dsx, gmat, s_own, s_sib, t_out, t_in, p_out, p_in, u_all, seg_out, seg_k, seg_q, bias_k, bias_q,
    kv_buf, q_buf, part_o, part_s, sib_o, sib_s, f_out, f_outs, f_in, f_ins, n_out, n_outs, n_in, n_ins, res,
    seg_sem, s_sem, t_ssem, t_rsem, p_ssem, p_rsem, h_sem, kv_sem, q_sem, sib_sem, chain_sem, out_sem,
):
    quads = len(modes)
    qs = [q for q in range(quads) if modes[q] == "q"]
    ks = [q for q in range(quads) if modes[q] == "k"]
    slices = quads * TILES
    chips = peers // 2
    owned = (slices + 1) // 2
    sec = lax.axis_index("section")
    me = lax.axis_index("seq")
    core = me % 2
    chip = me // 2
    sibling = me + 1 - 2 * core
    first = core == 0
    second = core == 1
    up2, up4 = me + 2 < peers, me + 4 < peers
    dn2, dn4 = me >= 2, me >= 4
    after_first = chip > 0
    before_last = chip < chips - 1

    def seq_dev(index):
        return (sec, index)

    def remote(src, dst, send, recv, device):
        return pltpu.make_async_remote_copy(
            src_ref=src, dst_ref=dst, send_sem=send, recv_sem=recv, device_id=device, device_id_type=MESH
        )

    def at(cond, fn):
        if cond is True:
            fn()
        else:
            pl.when(cond)(fn)

    pending = []

    def send(cond, copy):
        at(cond, copy.start)
        pending.append((cond, copy))

    def lane(j):
        return pl.ds(pl.multiple_of(j * LANES, LANES), LANES)

    def quad_lanes(q):
        return pl.ds(q * QUAD, QUAD)

    barrier = pltpu.get_barrier_semaphore()
    greeted = 0
    for hop in (1, sections - 1):
        pl.semaphore_signal(barrier, inc=1, device_id=((sec + hop) % sections, me), device_id_type=MESH)
        greeted += 1
    hops = sorted({2 * m for m in range(1, chips)} | {1, 3, peers - 3, peers - 1})
    for hop in hops:
        pl.semaphore_signal(barrier, inc=1, device_id=seq_dev((me + hop) % peers), device_id_type=MESH)
        greeted += 1
    pl.semaphore_wait(barrier, greeted)

    seg_out[...] = jnp.broadcast_to(seg_ref[...].astype(F32), (8, LANES))
    seg_copies = []
    for d in range(1, BACK + 1):
        fwd = remote(seg_out, seg_k.at[d - 1], seg_sem.at[0, d - 1], seg_sem.at[1, d - 1], seq_dev((me + d) % peers))
        bwd = remote(
            seg_out, seg_q.at[d - 1], seg_sem.at[2, d - 1], seg_sem.at[3, d - 1], seq_dev((me + peers - d) % peers)
        )
        send(True, fwd)
        send(True, bwd)
        seg_copies += [fwd, bwd]

    def kv_parts(q):
        n = ks.index(q)
        return [(n, w, (k_ref, v_ref)[w]) for w in range(2)]

    def kv_slot(n, w, d):
        return kv_buf.at[n, w, pl.ds(d * ROWS, ROWS)]

    def kv_copy(n, w, src, d, kind, device):
        return remote(src, kv_slot(n, w, d), kv_sem.at[0, n, w, kind], kv_sem.at[1, n, w, kind], seq_dev(device))

    right = (me + 2) % peers
    left = (me + peers - 2) % peers

    def kv_start(q):
        for n, w, src in kv_parts(q):
            own = src.at[:, quad_lanes(q)]
            send(up2, kv_copy(n, w, own, 2, 0, right))
            send(first, kv_copy(n, w, own, 1, 2, sibling))

    def kv_near(q):
        for n, w, _ in kv_parts(q):
            near = kv_slot(n, w, 2)
            at(dn2, kv_copy(n, w, near, 2, 0, right).wait_recv)
            send(dn2 & up2, kv_copy(n, w, near, 4, 1, right))
            send(dn2 & first, kv_copy(n, w, near, 3, 3, sibling))
            send(dn2 & second, kv_copy(n, w, near, 1, 2, sibling))

    def kv_far(q):
        for n, w, _ in kv_parts(q):
            far = kv_slot(n, w, 4)
            at(dn4, kv_copy(n, w, far, 4, 1, right).wait_recv)
            send(dn4 & second, kv_copy(n, w, far, 3, 3, sibling))

    def kv_last(q):
        for n, w, _ in kv_parts(q):
            at(second | dn2, kv_copy(n, w, kv_slot(n, w, 1), 1, 2, sibling).wait_recv)
            at((second & dn2) | (first & dn4), kv_copy(n, w, kv_slot(n, w, 3), 3, 3, sibling).wait_recv)

    for q in ks:
        kv_start(q)
    for n in range(len(ks)):
        for w in range(2):
            for d in range(1, BACK + 1):

                def blank(n=n, w=w, d=d):
                    kv_buf[n, w, pl.ds(d * ROWS, ROWS)] = jnp.zeros((ROWS, QUAD), BF16)

                at(me < d, blank)

    row_i, col_i = iota((ROWS, LANES), 0), iota((ROWS, LANES), 1)
    heads = rate_ref.shape[1]
    cum = dot((row_i >= col_i).astype(F32), rate_ref[...], precision=lax.Precision.HIGHEST)
    skip8 = jnp.broadcast_to(dskip_ref[...], (8, heads))
    bc = bc_ref[...]
    bc_t = bc.astype(F32).T
    b_t = bc_t[:NSTATE].astype(BF16)
    b_t2 = jnp.concatenate([b_t, b_t], axis=1)
    for q in range(quads):
        spread = (iota((heads, QUAD), 1) // HEAD_P + q * (QUAD // HEAD_P) == iota((heads, QUAD), 0)).astype(F32)
        cumx[:, quad_lanes(q)] = dot(cum, spread, precision=lax.Precision.HIGHEST)
        dsx[:, quad_lanes(q)] = dot(skip8, spread, precision=lax.Precision.HIGHEST)

        @pl.loop(q * TILES, (q + 1) * TILES)
        def _(j):
            sl = lane(j)
            cx = cumx[:, sl]
            total = cx[ROWS - 1 :]
            hi, lo = halves(x_ref[:, sl].astype(F32) * jnp.exp(cx - total))
            s_own[0:NSTATE, sl] = dot(b_t2, jnp.concatenate([hi, lo], axis=0))
            s_own[NSTATE : NSTATE + 8, sl] = jnp.broadcast_to(total, (8, LANES))

        send(
            True,
            remote(
                s_own.at[:, quad_lanes(q)], s_sib.at[:, quad_lanes(q)], s_sem.at[0, q], s_sem.at[1, q],
                seq_dev(sibling),
            ),
        )

    def t_copy(j):
        return remote(t_out.at[j // 2], t_in.at[chip], t_ssem.at[j // 2], t_rsem.at[chip], seq_dev(j))

    def states_out(q):
        quad = quad_lanes(q)
        remote(s_own.at[:, quad], s_sib.at[:, quad], s_sem.at[0, q], s_sem.at[1, q], seq_dev(sibling)).wait_recv()

        @pl.loop(q * TILES, (q + 1) * TILES)
        def _(j):
            @pl.when((j % 2 == core) & before_last)
            def _():
                sl = lane(j)
                own, sib = s_own[0:NSTATE, sl], s_sib[0:NSTATE, sl]
                own_tot, sib_tot = s_own[NSTATE : NSTATE + 1, sl], s_sib[NSTATE : NSTATE + 1, sl]
                early = jnp.where(first, own, sib)
                late = jnp.where(first, sib, own)
                late_tot = jnp.where(first, sib_tot, own_tot)
                both = jnp.exp(-late_tot) * early + late
                total = own_tot + sib_tot
                hi = total.astype(BF16).astype(F32)
                mid = (total - hi).astype(BF16).astype(F32)
                low = total - hi - mid
                place = iota((16, LANES), 0)
                tail = jnp.where(place == 0, hi, jnp.where(place == 1, mid, jnp.where(place == 2, low, 0.0)))
                block = jnp.concatenate([both, tail], axis=0).astype(BF16)

                @pl.when(j != me)
                def _():
                    t_out[j // 2] = block
                    t_copy(j).start()

                @pl.when(j == me)
                def _():
                    t_in[chip] = block

    def p_copy(owner, target):
        sl = lane(owner)
        return remote(
            p_out.at[target // 2], p_in.at[:, sl], p_ssem.at[target // 2], p_rsem.at[owner // 2], seq_dev(target)
        )

    def scan_states():
        @pl.when(me < slices)
        def _():
            def one(c, state):
                @pl.when((c != chip) & (c > 0))
                def _():
                    p_out[c] = state.astype(BF16)
                    p_copy(me, 2 * c + core).start()

                @pl.when(c == chip)
                def _():
                    p_in[:, lane(me)] = state.astype(BF16)

                @pl.when((c != chip) & (c < chips - 1))
                def _():
                    remote(t_out.at[0], t_in.at[c], t_ssem.at[0], t_rsem.at[c], seq_dev(me)).wait_recv()

                block = t_in[c].astype(F32)
                total = block[NSTATE : NSTATE + 1] + block[NSTATE + 1 : NSTATE + 2] + block[NSTATE + 2 : NSTATE + 3]
                return jnp.exp(-total) * state + block[:NSTATE]

            lax.fori_loop(0, chips, one, jnp.zeros((NSTATE, LANES), F32))

    def h_copy(j):
        return remote(p_in.at[:, lane(j)], p_in.at[:, lane(j)], h_sem.at[0, j], h_sem.at[1, j], seq_dev(sibling))

    def states_in(q):
        @pl.when(after_first)
        def _():
            @pl.loop(q * TILES, (q + 1) * TILES)
            def _(j):
                @pl.when(j % 2 == core)
                def _():
                    @pl.when(j != me)
                    def _():
                        p_copy(j, me).wait_recv()

                    h_copy(j).start()

            @pl.loop(q * TILES, (q + 1) * TILES)
            def _(j):
                @pl.when(j % 2 != core)
                def _():
                    h_copy(j).wait_recv()

    def init_states():
        @pl.when(jnp.logical_not(after_first))
        def _():
            p_in[...] = jnp.zeros_like(p_in)

    def local_y(q):
        t, r = row_i, col_i % HEAD_P
        left_half = col_i < HEAD_P

        @pl.loop(q * TILES, (q + 1) * TILES)
        def _(j):
            sl = lane(j)
            cx = cumx[:, sl]
            xs = x_ref[:, sl].astype(F32)
            mixes, blocks = [], []
            for part in range(2):
                rows = slice(part * HEAD_P, (part + 1) * HEAD_P)
                here = jnp.sum(
                    jnp.where(row_i[:HEAD_P] == r[:HEAD_P], cx[rows], 0.0), axis=0, keepdims=True
                )
                decay = jnp.exp(jnp.minimum(here - cx, 0.0))
                mixes.append(jnp.where(t >= r + part * HEAD_P, gmat[part] * decay, 0.0))
                blocks.append(jnp.where(left_half[:HEAD_P], xs[rows], 0.0))
                blocks.append(jnp.where(left_half[:HEAD_P], 0.0, xs[rows]))
            mixing = jnp.concatenate(mixes, axis=1).astype(BF16)
            inner = dot(mixing, jnp.concatenate(blocks, axis=0).astype(BF16))
            y0[:, sl] = inner + dsx[0:1, sl] * xs

    def make_u(q):
        c_only = bc_ref[:, NSTATE:]
        c2 = jnp.concatenate([c_only, c_only], axis=1)
        group = (iota((2 * LANES, LANES), 0) % LANES) // HEAD_P == iota((2 * LANES, LANES), 1) // HEAD_P
        ones = group.astype(F32).astype(BF16)

        @pl.loop(q * TILES, (q + 1) * TILES)
        def _(j):
            sl = lane(j)
            before = p_in[:, sl].astype(F32)
            after = jnp.exp(-s_sib[NSTATE : NSTATE + 1, sl]) * before + s_sib[0:NSTATE, sl]
            hi, lo = halves(jnp.where(first, before, after))
            carried = dot(c2, jnp.concatenate([hi, lo], axis=0))
            y = y0[:, sl] + carried * jnp.exp(-cumx[:, sl])
            hi, lo = halves(y * y)
            meansq = dot(jnp.concatenate([hi, lo], axis=1), ones) * (1.0 / HEAD_P)
            u = (y * lax.rsqrt(meansq + 1e-05) * gain_ref[:, sl]).astype(BF16)
            u_all[:, sl] = u

    lanes_w = {w: iota((ROWS, w), 1) for _, w in WINDOWS}
    heads4 = (iota((16, QUAD), 1) // ATT_DIM == iota((16, QUAD), 0) % 8).astype(F32).astype(BF16)
    scale = ATT_DIM ** (-0.5)
    sub8 = iota((8, LANES), 0)

    def only_head(a, block):
        start, width = WINDOWS[a]
        place = lanes_w[width] + start
        keep = (place >= a * ATT_DIM) & (place < (a + 1) * ATT_DIM)
        return jnp.where(keep, block.astype(F32), 0.0).astype(BF16)

    def joined(parts):
        tiles = []
        for tile in range(TILES):
            value = None
            for a, (start, width) in enumerate(WINDOWS):
                lo = tile * LANES - start
                if lo < 0 or lo >= width:
                    continue
                piece = parts[a][:, lo : lo + LANES]
                if value is None:
                    value = piece
                else:
                    value = jnp.where(col_i[:, :] + tile * LANES < a * ATT_DIM, value, piece)
            tiles.append(value)
        return tiles

    def spread4(rows8):
        hi, lo = halves(rows8)
        return dot(jnp.concatenate([hi, lo], axis=0), heads4, dims=((0,), (0,)))

    def finish(q, attended):
        sl = quad_lanes(q)
        res[:, sl] = (x_ref[:, sl].astype(F32) + u_all[:, sl].astype(F32) + attended).astype(BF16)
        send(
            True,
            remote(res.at[:, sl], out_ref.at[:, sl], out_sem.at[0, q], out_sem.at[1, q], ((sec + 1) % sections, me)),
        )

    def attend_kv(q):
        n = ks.index(q)
        base = q * QUAD
        for w, src in ((0, k_ref), (1, v_ref)):
            kv_buf[n, w, 0:ROWS] = src[:, quad_lanes(q)]
        outs = []
        inverse = jnp.zeros((8, LANES), F32)
        for a, (start, width) in enumerate(WINDOWS):
            mine = only_head(a, u_all[:, pl.ds(base + start, width)])
            score = dot(kv_buf[n, 0, :, start : start + width], mine, dims=((1,), (1,))) * scale + bias_k[...]
            top = jnp.max(score, axis=0, keepdims=True)
            expo = jnp.exp(score - top)
            inverse = jnp.where(sub8 == a, 1.0 / jnp.sum(expo, axis=0, keepdims=True), inverse)
            outs.append(dot(expo.astype(BF16), kv_buf[n, 1, :, start : start + width], dims=((0,), (0,))))
        finish(q, jnp.concatenate(joined(outs), axis=1) * spread4(inverse))

    def q_slot(n, d):
        return q_buf.at[n, pl.ds(d * ROWS, ROWS)]

    def q_copy(n, src, d, kind, device):
        return remote(src, q_slot(n, d), q_sem.at[0, n, kind], q_sem.at[1, n, kind], seq_dev(device))

    def q_start(q):
        n = qs.index(q)
        own = u_all.at[:, quad_lanes(q)]
        send(dn2, q_copy(n, own, 2, 0, left))
        send(second, q_copy(n, own, 1, 2, sibling))

    def q_near(q):
        n = qs.index(q)
        near = q_slot(n, 2)
        at(up2, q_copy(n, near, 2, 0, left).wait_recv)
        send(up2 & dn2, q_copy(n, near, 4, 1, left))
        send(up2 & second, q_copy(n, near, 3, 3, sibling))
        send(up2 & first, q_copy(n, near, 1, 2, sibling))

    def q_far(q):
        n = qs.index(q)
        far = q_slot(n, 4)
        at(up4, q_copy(n, far, 4, 1, left).wait_recv)
        send(up4 & first, q_copy(n, far, 3, 3, sibling))

    def q_last(q):
        n = qs.index(q)
        at(first | up2, q_copy(n, q_slot(n, 1), 1, 2, sibling).wait_recv)
        at((first & up2) | (second & up4), q_copy(n, q_slot(n, 3), 3, 3, sibling).wait_recv)

    def sib_copies(n, d, slot, kind):
        rows = pl.ds(d * ROWS, ROWS)
        return [
            remote(
                part_o.at[n, rows], sib_o.at[n, slot], sib_sem.at[0, n, kind, 0], sib_sem.at[1, n, kind, 0],
                seq_dev(sibling),
            ),
            remote(
                part_s.at[n, d], sib_s.at[n, slot], sib_sem.at[0, n, kind, 1], sib_sem.at[1, n, kind, 1],
                seq_dev(sibling),
            ),
        ]

    def partials(q):
        n = qs.index(q)
        base = q * QUAD
        q_buf[n, 0:ROWS] = u_all[:, quad_lanes(q)]

        @pl.loop(0, BACK + 1)
        def _(d):
            rows = pl.ds(pl.multiple_of(d * ROWS, ROWS), ROWS)
            outs = []
            tops, sums = jnp.zeros((8, LANES), F32), jnp.zeros((8, LANES), F32)
            for a, (start, width) in enumerate(WINDOWS):
                key = only_head(a, k_ref[:, pl.ds(base + start, width)])
                score = dot(key, q_buf[n, rows, start : start + width], dims=((1,), (1,))) * scale + bias_q[d]
                top = jnp.maximum(jnp.max(score, axis=0, keepdims=True), LOWEST)
                expo = jnp.exp(score - top)
                tops = jnp.where(sub8 == a, top, tops)
                sums = jnp.where(sub8 == a, jnp.sum(expo, axis=0, keepdims=True), sums)
                outs.append(dot(expo.astype(BF16), v_ref[:, pl.ds(base + start, width)], dims=((0,), (0,))))
            for tile, value in enumerate(joined(outs)):
                part_o[n, rows, tile * LANES : (tile + 1) * LANES] = value.astype(BF16)
            part_s[n, d, 0:8] = tops
            part_s[n, d, 8:16] = sums

        for kind, d in enumerate((1, 3)):
            for copy in sib_copies(n, d, core + kind, kind):
                send(True, copy)

    def sib_wait(q):
        n = qs.index(q)
        for kind, d in enumerate((1, 3)):
            for copy in sib_copies(n, d, 1 - core + kind, kind):
                copy.wait_recv()

    def merged(parts, final=False):
        top = functools.reduce(jnp.maximum, [s[0:8] for _, s in parts])
        weights = [jnp.exp(s[0:8] - top) for _, s in parts]
        total = sum(w * s[8:16] for w, (_, s) in zip(weights, parts))
        if final:
            inverse = jnp.where(sub8 < 4, 1.0 / jnp.where(sub8 < 4, total, 1.0), 0.0)
            weights = [w * inverse for w in weights]
        value = sum(spread4(w) * o.astype(F32) for w, (o, _) in zip(weights, parts))
        return value, top, total

    def part(n, d):
        return part_o[n, d * ROWS : (d + 1) * ROWS], part_s[n, d]

    def chain_copies(n, kind):
        src, srcs, dst, dsts = ((f_out, f_outs, f_in, f_ins), (n_out, n_outs, n_in, n_ins))[kind]
        return [
            remote(src.at[n], dst.at[n], chain_sem.at[0, n, kind, 0], chain_sem.at[1, n, kind, 0], seq_dev(right)),
            remote(srcs.at[n], dsts.at[n], chain_sem.at[0, n, kind, 1], chain_sem.at[1, n, kind, 1], seq_dev(right)),
        ]

    def send_far(q):
        n = qs.index(q)
        sib_wait(q)
        value, top, total = merged([part(n, 4), (sib_o[n, 2], sib_s[n, 2])])
        f_out[n] = value.astype(BF16)
        f_outs[n, 0:8] = top
        f_outs[n, 8:16] = total
        for copy in chain_copies(n, 0):
            send(up4, copy)

    def send_near(q):
        n = qs.index(q)
        for copy in chain_copies(n, 0):
            at(dn2 & up2, copy.wait_recv)
        value, top, total = merged([part(n, 2), (sib_o[n, 1], sib_s[n, 1]), (f_in[n], f_ins[n])])
        n_out[n] = value.astype(BF16)
        n_outs[n, 0:8] = top
        n_outs[n, 8:16] = total
        for copy in chain_copies(n, 1):
            send(up2, copy)

    def finish_q(q):
        n = qs.index(q)
        for copy in chain_copies(n, 1):
            at(dn2, copy.wait_recv)
        value, _, _ = merged([part(n, 0), (sib_o[n, 0], sib_s[n, 0]), (n_in[n], n_ins[n])], final=True)
        finish(q, value)

    def blank_results():
        nothing = jnp.where(iota((16, LANES), 0) < 8, LOWEST, 0.0)

        @pl.loop(0, len(qs))
        def _(n):
            @pl.when(first)
            def _():
                sib_o[n, 0] = jnp.zeros((ROWS, QUAD), BF16)
                sib_s[n, 0] = nothing

            @pl.when(second)
            def _():
                sib_o[n, 2] = jnp.zeros((ROWS, QUAD), BF16)
                sib_s[n, 2] = nothing

            @pl.when(jnp.logical_not(dn2))
            def _():
                f_in[n] = jnp.zeros((ROWS, QUAD), BF16)
                f_ins[n] = nothing
                n_in[n] = jnp.zeros((ROWS, QUAD), BF16)
                n_ins[n] = nothing

    def masks():
        for copy in seg_copies:
            copy.wait_recv()
        own = jnp.broadcast_to(seg_out[0:1], (ROWS, LANES))
        own_col = own.T
        for d in range(BACK + 1):
            if d == 0:
                keep_q = keep_k = (own_col == own) & (row_i <= col_i)
            else:
                other_q = jnp.broadcast_to(seg_q[d - 1, 0:1], (ROWS, LANES))
                other_k = jnp.broadcast_to(seg_k[d - 1, 0:1], (ROWS, LANES)).T
                keep_q = (own_col == other_q) & (me + d < peers)
                keep_k = (other_k == own) & (me >= d)
            bias_q[d] = jnp.where(keep_q, 0.0, MASKED)
            bias_k[d * ROWS : (d + 1) * ROWS] = jnp.where(keep_k, 0.0, MASKED)

    for q in range(quads):
        states_out(q)
    b_only = bc_ref[:, :NSTATE]
    c_only = bc_ref[:, NSTATE:]
    for part_no in range(2):
        rows = b_only[part_no * HEAD_P : (part_no + 1) * HEAD_P]
        gmat[part_no] = dot(c_only, jnp.concatenate([rows, rows], axis=0), dims=((1,), (1,)))
    init_states()
    local_y(0)
    scan_states()
    for q in range(1, quads):
        local_y(q)
    masks()
    if qs:
        blank_results()
    for q in ks:
        kv_near(q)

    order = qs + ks
    for place, q in enumerate(order):
        states_in(q)
        make_u(q)
        if q in qs:
            if place:
                q_near(qs[place - 1])
            q_start(q)
    for q in ks:
        kv_far(q)
    for place, q in enumerate(qs):
        if place == len(qs) - 1:
            q_near(q)
        q_far(q)
        q_last(q)
        partials(q)
        send_far(q)
        if place >= 1:
            send_near(qs[place - 1])
        if place >= 2:
            finish_q(qs[place - 2])
    for q in ks:
        kv_last(q)
        attend_kv(q)
    if qs:
        send_near(qs[-1])
        for q in qs[-2:]:
            finish_q(q)

    for q in range(quads):
        sl = quad_lanes(q)
        remote(res.at[:, sl], out_ref.at[:, sl], out_sem.at[0, q], out_sem.at[1, q], (sec, me)).wait_recv()
    for cond, copy in pending:
        at(cond, copy.wait_send)

    @pl.loop(0, slices)
    def _(j):
        @pl.when(j % 2 == core)
        def _():
            @pl.when(before_last & (j != me))
            def _():
                t_copy(j).wait_send()

            @pl.when(after_first)
            def _():
                h_copy(j).wait_send()

    @pl.when(me < slices)
    def _():
        @pl.loop(1, chips)
        def _(c):
            @pl.when(c != chip)
            def _():
                p_copy(me, 2 * c + core).wait_send()


def layer(modes, sections, peers, x, k, v, bc, rates, dskip, gain, seg):
    quads = len(modes)
    width = quads * QUAD
    slices = quads * TILES
    owned = (slices + 1) // 2
    chips = peers // 2
    nq = max(1, modes.count("q"))
    nk = max(1, modes.count("k"))
    dma = pltpu.SemaphoreType.DMA
    block = (ROWS, QUAD)
    scratch = [
        pltpu.VMEM((ROWS, width), F32),
        pltpu.VMEM((ROWS, width), F32),
        pltpu.VMEM((8, width), F32),
        pltpu.VMEM((2, ROWS, LANES), F32),
        pltpu.VMEM((NSTATE + 8, width), F32),
        pltpu.VMEM((NSTATE + 8, width), F32),
        pltpu.VMEM((owned, NSTATE + 16, LANES), BF16),
        pltpu.VMEM((chips, NSTATE + 16, LANES), BF16),
        pltpu.VMEM((chips, NSTATE, LANES), BF16),
        pltpu.VMEM((NSTATE, width), BF16),
        pltpu.VMEM((ROWS, width), BF16),
        pltpu.VMEM((8, LANES), F32),
        pltpu.VMEM((BACK, 8, LANES), F32),
        pltpu.VMEM((BACK, 8, LANES), F32),
        pltpu.VMEM((SPAN, LANES), F32),
        pltpu.VMEM((BACK + 1, ROWS, LANES), F32),
        pltpu.VMEM((nk, 2, SPAN, QUAD), BF16),
        pltpu.VMEM((nq, SPAN, QUAD), BF16),
        pltpu.VMEM((nq, SPAN, QUAD), BF16),
        pltpu.VMEM((nq, BACK + 1, 16, LANES), F32),
        pltpu.VMEM((nq, 3) + block, BF16),
        pltpu.VMEM((nq, 3, 16, LANES), F32),
    ]
    for _ in range(4):
        scratch += [pltpu.VMEM((nq,) + block, BF16), pltpu.VMEM((nq, 16, LANES), F32)]
    scratch += [
        pltpu.VMEM((ROWS, width), BF16),
        dma((4, BACK)),
        dma((2, quads)),
        dma((owned,)),
        dma((chips,)),
        dma((chips,)),
        dma((owned,)),
        dma((2, slices)),
        dma((2, nk, 2, 4)),
        dma((2, nq, 4)),
        dma((2, nq, 2, 2)),
        dma((2, nq, 2, 2)),
        dma((2, quads)),
    ]
    vmem = pl.BlockSpec(memory_space=pltpu.VMEM)
    return pl.pallas_call(
        functools.partial(kernel, modes, sections, peers),
        out_shape=jax.ShapeDtypeStruct((ROWS, width), BF16),
        in_specs=[vmem] * 8,
        out_specs=pl.BlockSpec(memory_space=pl.ANY),
        scratch_shapes=scratch,
        compiler_params=pltpu.CompilerParams(
            collective_id=0, has_side_effects=True, vmem_limit_bytes=56 * 1024 * 1024
        ),
        name="layer",
    )(x, k, v, bc, rates, dskip, gain, seg)


def build(mesh, modes):
    sections, peers = mesh.shape["section"], mesh.shape["seq"]

    def body(stream, keys, values, bc, rates, dskip, norm_gain, seg_ids):
        out = layer(
            modes, sections, peers,
            stream[0], keys[0], values[0], bc[0], rates[0], dskip, norm_gain, seg_ids,
        )
        return out[None]

    rows = P("section", "seq", None)
    return jax.shard_map(
        body,
        mesh=mesh,
        in_specs=(rows, rows, rows, rows, rows, P("section", None), P("section", None), P("section", "seq")),
        out_specs=rows,
        check_vma=False,
    )


def solution(mesh):
    return build(mesh, MODES)
```
